256 devices in a mesh: lvl: 32 (over z, x), blk: 8 (over y, core).
Axes of the slice: x: 4, y: 4, z: 8, core: 2. Of those that a mesh axis runs over, the one named last changes fastest.
Arguments:
- right_sides: bfloat16 [8, 131072, 256], P('blk', 'lvl'), may hold values from -6 to 6
- row_vectors: bfloat16 [131072, 256], P('lvl'), may hold values from -6 to 6
- leaf_basis_in: bfloat16 [8, 1024, 128, 64], P('blk', 'lvl'), may hold values from -0.5 to 0.5
- leaf_basis_out: bfloat16 [8, 1024, 128, 64], P('blk', 'lvl'), may hold values from -0.75 to 0.75
- transfers: bfloat16 [8, 10, 1024, 2, 64, 64], P('blk', None, 'lvl'), may hold values from -0.625 to 0.625
- tile_ranks: int32 [8, 11, 1024], P('blk', None, 'lvl'), may hold values from 32 to 64, as said below
Outputs:
- row_result: bfloat16 [131072, 256], P(('lvl', 'blk'))
- column_result: bfloat16 [8, 131072, 256], P('blk', 'lvl')
The draws below stay inside these ranges and needn't reach their ends.
Inputs may be any that keep to these rules, and one draw needn't show every extreme that they name: `tile_ranks`: every entry is 32 or 64, and both occur.
All inputs are finite; a program needn't handle non-finite values.
Results may differ from the reference program's by a relative error of at most 0.027.
Values may be sent and summed in bfloat16 or wider, within the bound.
A program may use at most 128 MiB of HBM per device.

```python
import jax
import jax.numpy as jnp

LEVELS = 10
LEAF = 128
RANK = 64
NRHS = 256
NLEAF = 1024
COLS = 131072
BLOCKS = 8


def draw_tile_ranks(key, part):
    choose = jax.random.randint(key, (BLOCKS, LEVELS + 1, NLEAF), 0, 2)
    values = (choose + 1) * (RANK // 2)
    values = values.at[0, 0, 0].set(RANK)
    values = values.at[0, 0, 1].set(RANK // 2)
    return values.astype(jnp.int32)


def block_levels(rng, shape, split, least, top_value):
    loudness, own = 1.0, jax.random.fold_in(rng, 6)
    for axis_at, blocks in split:
        steps = jnp.exp(jax.random.uniform(jax.random.fold_in(own, axis_at), (blocks,), jnp.float32, least / len(split), top_value / len(split)))
        loudness = loudness * jnp.repeat(steps, shape[axis_at] // blocks).reshape([-1 if axis == axis_at else 1 for axis in range(len(shape))])
    return loudness


def bell_draw(stream_key, shape, deviation, reach, shards=(), kind=jnp.bfloat16):
    values = deviation * jax.random.normal(stream_key, shape, jnp.float32)
    if shards:
        values = values * block_levels(stream_key, shape, shards, -0.22, 0.18)
    return jnp.clip(values, -reach, reach).astype(kind)


def setup_inputs(seed: int = 0) -> dict:
    streams_of = jax.random.split(jax.random.key(seed), 7)
    return {
        "right_sides": bell_draw(streams_of[0], (BLOCKS, COLS, NRHS), 1.0, 6.0, ((0, 8), (1, 32))),
        "row_vectors": bell_draw(streams_of[1], (COLS, NRHS), 1.0, 6.0, ((0, 32),)),
        "leaf_basis_in": bell_draw(streams_of[2], (BLOCKS, NLEAF, LEAF, RANK), LEAF ** -0.5, 0.5, ((0, 8), (1, 32))),
        "leaf_basis_out": bell_draw(streams_of[3], (BLOCKS, NLEAF, LEAF, RANK), RANK ** -0.5, 0.75, ((0, 8), (1, 32))),
        "transfers": bell_draw(streams_of[4], (BLOCKS, LEVELS, NLEAF, 2, RANK, RANK), (3 * RANK // 2) ** -0.5, 0.625, ((0, 8), (2, 32))),
        "tile_ranks": draw_tile_ranks(jax.random.fold_in(streams_of[6], 71), 0),
    }


def rank_grid(rank_row, height):
    span_rows = 2 ** height
    span_cols = 2 ** (LEVELS - height)
    if height <= LEVELS // 2:
        return rank_row.reshape(span_cols, span_rows).T
    return rank_row.reshape(span_rows, span_cols)


def rank_mask(values, rank_table):
    inside = jnp.arange(values.shape[2]).astype(jnp.int32)[None, None, :, None] < rank_table[:, :, None, None]
    return jnp.where(inside, values, jnp.zeros_like(values))


def level_tiles(tile_level, height):
    span_rows = 2 ** height
    span_cols = 2 ** (LEVELS - height)
    if height <= LEVELS // 2:
        grid = tile_level.reshape(span_cols, span_rows, 2, RANK, RANK).transpose(1, 0, 2, 3, 4)
    else:
        grid = tile_level.reshape(span_rows, span_cols, 2, RANK, RANK)
    return grid.reshape(span_rows // 2, 2, span_cols, 2, RANK, RANK).astype(jnp.float32)


def forward_block(right_block, basis_in, basis_out, tile_block, rank_block):
    leaf_rows = right_block.reshape(NLEAF, LEAF, NRHS).astype(jnp.float32)
    coefficients = jnp.einsum('nlr,nlk->nrk', basis_in.astype(jnp.float32), leaf_rows)[None]
    coefficients = rank_mask(coefficients, rank_grid(rank_block[0], 0)).astype(jnp.bfloat16)
    for height in range(1, LEVELS + 1):
        span_rows = 2 ** height
        span_cols = 2 ** (LEVELS - height)
        grid = level_tiles(tile_block[height - 1], height)
        before = coefficients.reshape(span_rows // 2, span_cols, 2, RANK, NRHS).astype(jnp.float32)
        updated = jnp.einsum('hbjcrs,hjcsk->hbjrk', grid, before).reshape(span_rows, span_cols, RANK, NRHS)
        coefficients = rank_mask(updated, rank_grid(rank_block[height], height)).astype(jnp.bfloat16)
    block_part = jnp.einsum('nlr,nrk->nlk', basis_out.astype(jnp.float32), coefficients[:, 0].astype(jnp.float32))
    return block_part.astype(jnp.bfloat16).reshape(COLS, NRHS)


def adjoint_block(row_vectors, basis_in, basis_out, tile_block, rank_block):
    leaf_rows = row_vectors.reshape(NLEAF, LEAF, NRHS).astype(jnp.float32)
    adjoint = jnp.einsum('nlr,nlk->nrk', basis_out.astype(jnp.float32), leaf_rows)[:, None]
    adjoint = rank_mask(adjoint, rank_grid(rank_block[LEVELS], LEVELS)).astype(jnp.bfloat16)
    for height in range(LEVELS, 0, -1):
        span_rows = 2 ** height
        span_cols = 2 ** (LEVELS - height)
        grid = level_tiles(tile_block[height - 1], height)
        current = adjoint.reshape(span_rows // 2, 2, span_cols, RANK, NRHS).astype(jnp.float32)
        updated = jnp.einsum('hbjcrs,hbjrk->hjcsk', grid, current).reshape(span_rows // 2, 2 * span_cols, RANK, NRHS)
        adjoint = rank_mask(updated, rank_grid(rank_block[height - 1], height - 1)).astype(jnp.bfloat16)
    result = jnp.einsum('nlr,nrk->nlk', basis_in.astype(jnp.float32), adjoint[0].astype(jnp.float32))
    return result.astype(jnp.bfloat16).reshape(COLS, NRHS)


def reference(right_sides, row_vectors, leaf_basis_in, leaf_basis_out, transfers, tile_ranks):
    total = jnp.zeros((COLS, NRHS), jnp.float32)
    columns = []
    for block_index in range(BLOCKS):
        block_part = forward_block(right_sides[block_index], leaf_basis_in[block_index], leaf_basis_out[block_index], transfers[block_index], tile_ranks[block_index])
        total = total + block_part.astype(jnp.float32)
        columns.append(adjoint_block(row_vectors, leaf_basis_in[block_index], leaf_basis_out[block_index], transfers[block_index], tile_ranks[block_index]))
    return (total.astype(jnp.bfloat16), jnp.stack(columns, axis=0))
```

```python
import jax
import jax.numpy as jnp
from jax import lax
from jax.experimental import pallas as pl
from jax.experimental.pallas import tpu as pltpu
from jax.sharding import PartitionSpec as P

LEVELS = 10
MIDDLE = LEVELS // 2
LEAF = 128
RANK = 64
HALF = RANK // 2
NRHS = 256
NODES = 32
PAIRS = NODES // 2
GROUPS = 8
CHIPS = GROUPS // 2
SHARE = NODES // GROUPS
UNROLL = 4
MESH = pl.DeviceIdType.MESH
F32 = jnp.float32
BF16 = jnp.bfloat16


def kernel(
    right_hbm, rows_hbm, basis_in_hbm, basis_out_hbm, tiles_hbm, ranks,
    row_out, col_out,
    right, rows, basis_in, basis_out, tiles, ping, pong,
    send_f, recv_f, send_a, recv_a,
    part, swap, pair_sum, gathered, row_buf, col_buf,
    load_sem, tile_sem, store_sem, row_sem,
    ssem_f, rsem_f, ssem_a, rsem_a, ssem_c, rsem_c, ssem_y, rsem_y,
):
    me = lax.axis_index("lvl")
    blk = lax.axis_index("blk")
    core = lax.rem(blk, 2)
    chip = blk // 2
    my_pair = me // 2

    quarter = NODES // 4
    loads = {}
    for name, src, dst, base in (
        ("right", right_hbm, right, 0),
        ("rows", rows_hbm, rows, 4),
        ("basis_in", basis_in_hbm, basis_in, 8),
        ("basis_out", basis_out_hbm, basis_out, 9),
    ):
        if base < 8:
            loads[name] = [
                pltpu.make_async_copy(
                    src.at[pl.ds(c * quarter, quarter)],
                    dst.at[pl.ds(c * quarter, quarter)],
                    load_sem.at[base + c],
                )
                for c in range(4)
            ]
        else:
            loads[name] = [pltpu.make_async_copy(src, dst, load_sem.at[base])]
    tile_loads = [
        pltpu.make_async_copy(tiles_hbm.at[l], tiles.at[l], tile_sem.at[l]) for l in range(LEVELS)
    ]
    for copy in loads["basis_in"] + loads["right"] + tile_loads[:MIDDLE]:
        copy.start()
    for copy in loads["basis_out"] + loads["rows"] + tile_loads[: MIDDLE - 1 : -1]:
        copy.start()

    barrier = pltpu.get_barrier_semaphore()

    def greet(k, carry):
        pl.semaphore_signal(
            barrier, inc=1, device_id=(lax.rem(me + k, NODES), blk), device_id_type=MESH
        )
        return carry

    lax.fori_loop(1, NODES, greet, 0)
    for k in range(1, CHIPS):
        other = lax.rem(chip + k, CHIPS) * 2 + core
        pl.semaphore_signal(barrier, inc=1, device_id=(me, other), device_id_type=MESH)
    pl.semaphore_signal(
        barrier, inc=1, device_id=(me, chip * 2 + 1 - core), device_id_type=MESH
    )

    def loop(count, body, unroll=UNROLL):
        def step(t, carry):
            for u in range(unroll):
                body(t * unroll + u)
            return carry

        lax.fori_loop(0, count // unroll, step, 0)

    def keep(level, node, values):
        return jnp.where(ranks[level, 0, node] > HALF, values, jnp.zeros_like(values))

    def put_node(ref, node, values, level=None, rank_node=None):
        ref[node, 0:HALF] = values[0:HALF].astype(BF16)
        low = values[HALF:RANK]
        if level is not None:
            low = keep(level, rank_node, low)
        ref[node, HALF:RANK] = low.astype(BF16)

    def matrix(level, first, second):
        t = tiles
        return jnp.concatenate(
            [
                jnp.concatenate([t[level - 1, node, 0], t[level - 1, node, 1]], axis=1)
                for node in (first, second)
            ],
            axis=0,
        )

    def two(ref, first, second):
        return jnp.concatenate([ref[first], ref[second]], axis=0)

    def apply(w, x):
        return jnp.dot(w, x, preferred_element_type=F32)

    def apply_t(w, x):
        return lax.dot_general(w, x, (((0,), (0,)), ((), ())), preferred_element_type=F32)

    def copy_f(q, node):
        return pltpu.make_async_remote_copy(
            send_f.at[q], recv_f.at[node], ssem_f.at[q], rsem_f.at[node],
            device_id=(q, blk), device_id_type=MESH,
        )

    def copy_a(q, node):
        return pltpu.make_async_remote_copy(
            send_a.at[q], recv_a.at[node], ssem_a.at[q], rsem_a.at[node],
            device_id=(q, blk), device_id_type=MESH,
        )

    def hand_over(q, send, recv, copy):
        @pl.when(q != me)
        def _():
            copy(q, me).start()

        @pl.when(q == me)
        def _():
            recv[me] = send[q]

    def arrived(q, copy):
        @pl.when(q != me)
        def _():
            copy(q, q).wait_recv()

    loads["basis_in"][0].wait()
    for c in range(4):
        loads["right"][c].wait()

        def leaf(n, c=c):
            n = c * quarter + n
            put_node(ping, n, apply(basis_in[n], right[n]), 0, n)

        loop(quarter, leaf)
    src, dst = ping, pong
    for level in range(1, MIDDLE):
        tile_loads[level - 1].wait()
        span = 2 ** (level - 1)

        def low(t, level=level, span=span, src=src, dst=dst):
            j, h = t // span, lax.rem(t, span)
            at = 2 * j * span + h
            out = apply(matrix(level, 2 * t, 2 * t + 1), two(src, at, at + span))
            put_node(dst, 2 * t, out[:RANK], level, 2 * t)
            put_node(dst, 2 * t + 1, out[RANK:], level, 2 * t + 1)

        loop(PAIRS, low)
        src, dst = dst, src
    tile_loads[MIDDLE - 1].wait()
    pl.semaphore_wait(barrier, NODES - 1 + CHIPS)

    def low_last(k, src=src):
        h = jnp.bitwise_xor(my_pair, k)
        out = apply(matrix(MIDDLE, 2 * h, 2 * h + 1), two(src, h, h + PAIRS))
        put_node(send_f, 2 * h, out[:RANK], MIDDLE, 2 * h)
        put_node(send_f, 2 * h + 1, out[RANK:], MIDDLE, 2 * h + 1)
        hand_over(2 * h, send_f, recv_f, copy_f)
        hand_over(2 * h + 1, send_f, recv_f, copy_f)

    loop(PAIRS, low_last, 2)

    loads["basis_out"][0].wait()
    for c in range(4):
        loads["rows"][c].wait()

        def row_leaf(n, c=c):
            n = c * quarter + n
            put_node(ping, n, apply(basis_out[n], rows[n]), LEVELS, n)

        loop(quarter, row_leaf)
    src, dst = ping, pong
    for level in range(LEVELS, MIDDLE + 1, -1):
        tile_loads[level - 1].wait()
        width = 2 ** (LEVELS - level)

        def high_t(u, level=level, width=width, src=src, dst=dst):
            h, j = u // width, lax.rem(u, width)
            first = 2 * h * width + j
            out = apply_t(matrix(level, first, first + width), two(src, first, first + width))
            put_node(dst, 2 * u, out[:RANK], level - 1, 2 * u)
            put_node(dst, 2 * u + 1, out[RANK:], level - 1, 2 * u + 1)

        loop(PAIRS, high_t)
        src, dst = dst, src
    tile_loads[MIDDLE].wait()

    def high_t_last(k, src=src):
        j = jnp.bitwise_xor(my_pair, k)
        out = apply_t(matrix(MIDDLE + 1, j, j + PAIRS), two(src, j, j + PAIRS))
        put_node(send_a, 2 * j, out[:RANK])
        put_node(send_a, 2 * j + 1, out[RANK:])
        hand_over(2 * j, send_a, recv_a, copy_a)
        hand_over(2 * j + 1, send_a, recv_a, copy_a)

    loop(PAIRS, high_t_last, 2)

    def high_first(k, dst=ping):
        j = jnp.bitwise_xor(my_pair, k)
        arrived(2 * j, copy_f)
        arrived(2 * j + 1, copy_f)
        out = apply(matrix(MIDDLE + 1, j, j + PAIRS), two(recv_f, 2 * j, 2 * j + 1))
        put_node(dst, j, out[:RANK], MIDDLE + 1, j)
        put_node(dst, j + PAIRS, out[RANK:], MIDDLE + 1, j + PAIRS)

    loop(PAIRS, high_first, 2)
    src, dst = ping, pong
    for level in range(MIDDLE + 2, LEVELS + 1):
        width = 2 ** (LEVELS - level)

        def high(u, level=level, width=width, src=src, dst=dst):
            h, j = u // width, lax.rem(u, width)
            first = 2 * h * width + j
            out = apply(matrix(level, first, first + width), two(src, 2 * u, 2 * u + 1))
            put_node(dst, first, out[:RANK], level, first)
            put_node(dst, first + width, out[RANK:], level, first + width)

        loop(PAIRS, high)
        src, dst = dst, src

    def swap_copy(y):
        group = 2 * y + 1 - core
        return pltpu.make_async_remote_copy(
            part.at[pl.ds(SHARE * group, SHARE)], swap.at[y], ssem_c.at[y], rsem_c.at[y],
            device_id=(me, chip * 2 + 1 - core), device_id_type=MESH,
        )

    def y_copy(y, slot):
        return pltpu.make_async_remote_copy(
            pair_sum.at[y], gathered.at[slot], ssem_y.at[y], rsem_y.at[slot],
            device_id=(me, 2 * y + core), device_id_type=MESH,
        )

    def row_leaf_out(group, src=src):
        for s in range(SHARE):
            n = SHARE * group + s
            part[n] = apply_t(basis_out[n], src[n]).astype(BF16)

    def for_sibling(y, carry):
        row_leaf_out(2 * y + 1 - core)
        swap_copy(y).start()
        return carry

    lax.fori_loop(0, CHIPS, for_sibling, 0)

    def for_core(y, carry):
        row_leaf_out(2 * y + core)
        return carry

    lax.fori_loop(0, CHIPS, for_core, 0)

    def exchange(k, carry):
        y = lax.rem(chip + k, CHIPS)
        swap_copy(y).wait_recv()
        group = 2 * y + core
        for s in range(SHARE):
            pair_sum[y, s] = (
                part[SHARE * group + s].astype(F32) + swap[y, s].astype(F32)
            ).astype(BF16)

        @pl.when(y != chip)
        def _():
            y_copy(y, chip).start()

        return carry

    lax.fori_loop(1, CHIPS + 1, exchange, 0)

    def low_t_first(k, dst=ping):
        h = jnp.bitwise_xor(my_pair, k)
        arrived(2 * h, copy_a)
        arrived(2 * h + 1, copy_a)
        pieces = []
        for node in (2 * h, 2 * h + 1):
            pieces.append(recv_a[node, 0:HALF])
            pieces.append(keep(MIDDLE, node, recv_a[node, HALF:RANK]))
        out = apply_t(matrix(MIDDLE, 2 * h, 2 * h + 1), jnp.concatenate(pieces, axis=0))
        put_node(dst, h, out[:RANK], MIDDLE - 1, h)
        put_node(dst, h + PAIRS, out[RANK:], MIDDLE - 1, h + PAIRS)

    loop(PAIRS, low_t_first, 2)

    for k in range(1, CHIPS):
        y = lax.rem(chip + k, CHIPS)
        y_copy(y, y).wait_recv()
    for s in range(SHARE):
        total = pair_sum[chip, s].astype(F32)
        for k in range(1, CHIPS):
            total = total + gathered[lax.rem(chip + k, CHIPS), s].astype(F32)
        row_buf[s] = total.astype(BF16)
    row_store = pltpu.make_async_copy(row_buf, row_out, row_sem)
    row_store.start()

    src, dst = ping, pong
    for level in range(MIDDLE - 1, 0, -1):
        span = 2 ** (level - 1)

        def low_t(t, level=level, span=span, src=src, dst=dst):
            j, h = t // span, lax.rem(t, span)
            at = 2 * j * span + h
            out = apply_t(matrix(level, 2 * t, 2 * t + 1), two(src, 2 * t, 2 * t + 1))
            put_node(dst, at, out[:RANK], level - 1, at)
            put_node(dst, at + span, out[RANK:], level - 1, at + span)

        loop(PAIRS, low_t)
        src, dst = dst, src
    stores = []
    for c in range(4):

        def leaf_out(n, c=c, src=src):
            n = c * quarter + n
            col_buf[n] = apply_t(basis_in[n], src[n]).astype(BF16)

        loop(quarter, leaf_out)
        stores.append(
            pltpu.make_async_copy(
                col_buf.at[pl.ds(c * quarter, quarter)],
                col_out.at[pl.ds(c * quarter, quarter)],
                store_sem.at[c],
            )
        )
        stores[-1].start()

    def sent(k, carry):
        q = lax.rem(me + k, NODES)
        copy_f(q, me).wait_send()
        copy_a(q, me).wait_send()
        return carry

    lax.fori_loop(1, NODES, sent, 0)
    for y in range(CHIPS):
        swap_copy(y).wait_send()
    for k in range(1, CHIPS):
        y_copy(lax.rem(chip + k, CHIPS), chip).wait_send()
    for copy in stores:
        copy.wait()
    row_store.wait()


def body(right_sides, row_vectors, leaf_basis_in, leaf_basis_out, transfers, tile_ranks):
    hbm = pl.BlockSpec(memory_space=pl.ANY)
    nodes = (NODES, RANK, NRHS)
    leaves = (NODES, LEAF, NRHS)
    dma = pltpu.SemaphoreType.DMA
    row, col = pl.pallas_call(
        kernel,
        out_shape=(
            jax.ShapeDtypeStruct((SHARE, LEAF, NRHS), BF16),
            jax.ShapeDtypeStruct(leaves, BF16),
        ),
        in_specs=[hbm] * 5 + [pl.BlockSpec(memory_space=pltpu.SMEM)],
        out_specs=(hbm, hbm),
        scratch_shapes=[
            pltpu.VMEM(leaves, BF16),
            pltpu.VMEM(leaves, BF16),
            pltpu.VMEM((NODES, RANK, LEAF), BF16),
            pltpu.VMEM((NODES, RANK, LEAF), BF16),
            pltpu.VMEM((LEVELS, NODES, 2, RANK, RANK), BF16),
            pltpu.VMEM(nodes, BF16),
            pltpu.VMEM(nodes, BF16),
            pltpu.VMEM(nodes, BF16),
            pltpu.VMEM(nodes, BF16),
            pltpu.VMEM(nodes, BF16),
            pltpu.VMEM(nodes, BF16),
            pltpu.VMEM(leaves, BF16),
            pltpu.VMEM((CHIPS, SHARE, LEAF, NRHS), BF16),
            pltpu.VMEM((CHIPS, SHARE, LEAF, NRHS), BF16),
            pltpu.VMEM((CHIPS, SHARE, LEAF, NRHS), BF16),
            pltpu.VMEM((SHARE, LEAF, NRHS), BF16),
            pltpu.VMEM(leaves, BF16),
            dma((10,)),
            dma((LEVELS,)),
            dma((4,)),
            dma,
            dma((NODES,)),
            dma((NODES,)),
            dma((NODES,)),
            dma((NODES,)),
            dma((CHIPS,)),
            dma((CHIPS,)),
            dma((CHIPS,)),
            dma((CHIPS,)),
        ],
        compiler_params=pltpu.CompilerParams(
            collective_id=0, has_side_effects=True, vmem_limit_bytes=56 << 20
        ),
        name="butterfly",
    )(
        right_sides.reshape(leaves),
        row_vectors.reshape(leaves),
        jnp.swapaxes(leaf_basis_in[0], 1, 2),
        jnp.swapaxes(leaf_basis_out[0], 1, 2),
        transfers[0],
        jnp.swapaxes(tile_ranks, 0, 1),
    )
    return row.reshape(SHARE * LEAF, NRHS), col.reshape(1, NODES * LEAF, NRHS)


def solution(mesh):
    return jax.shard_map(
        body,
        mesh=mesh,
        in_specs=(
            P("blk", "lvl", None),
            P("lvl", None),
            P("blk", "lvl", None, None),
            P("blk", "lvl", None, None),
            P("blk", None, "lvl", None, None, None),
            P("blk", None, "lvl"),
        ),
        out_specs=(P(("lvl", "blk"), None), P("blk", "lvl", None)),
        check_vma=False,
    )
```

```python
import jax
import jax.numpy as jnp
from jax import lax
from jax.experimental import pallas as pl
from jax.experimental.pallas import tpu as pltpu
from jax.sharding import PartitionSpec as P

LEVELS = 10
MIDDLE = LEVELS // 2
LEAF = 128
RANK = 64
HALF = RANK // 2
NRHS = 256
NODES = 32
PAIRS = NODES // 2
GROUPS = 8
CHIPS = GROUPS // 2
SHARE = NODES // GROUPS
MESH = pl.DeviceIdType.MESH
F32 = jnp.float32
BF16 = jnp.bfloat16


def kernel(
    right_hbm, rows_hbm, basis_in, basis_out, tiles_hbm, ranks,
    row_out, col_out,
    right, rows, tiles, turned, ping, pong,
    send_f, recv_f, send_a, recv_a,
    part, swap, pair_sum, gathered,
    load_sem, tile_sem,
    ssem_f, rsem_f, ssem_a, rsem_a, ssem_c, rsem_c, ssem_y, rsem_y,
):
    me = lax.axis_index("lvl")
    blk = lax.axis_index("blk")
    core = lax.rem(blk, 2)
    chip = blk // 2
    my_pair = me // 2

    quarter = NODES // 4
    loads = {}
    for name, src, dst, base in (("right", right_hbm, right, 0), ("rows", rows_hbm, rows, 4)):
        loads[name] = [
            pltpu.make_async_copy(
                src.at[pl.ds(c * quarter, quarter)],
                dst.at[pl.ds(c * quarter, quarter)],
                load_sem.at[base + c],
            )
            for c in range(4)
        ]
    tile_loads = [
        pltpu.make_async_copy(tiles_hbm.at[l], tiles.at[l], tile_sem.at[l]) for l in range(LEVELS)
    ]
    for copy in loads["right"] + tile_loads[:MIDDLE]:
        copy.start()
    for copy in loads["rows"] + tile_loads[: MIDDLE - 1 : -1]:
        copy.start()

    barrier = pltpu.get_barrier_semaphore()

    def greet(k, carry):
        pl.semaphore_signal(
            barrier, inc=1, device_id=(lax.rem(me + k, NODES), blk), device_id_type=MESH
        )
        return carry

    lax.fori_loop(1, NODES, greet, 0)
    for k in range(1, CHIPS):
        other = lax.rem(chip + k, CHIPS) * 2 + core
        pl.semaphore_signal(barrier, inc=1, device_id=(me, other), device_id_type=MESH)
    pl.semaphore_signal(
        barrier, inc=1, device_id=(me, chip * 2 + 1 - core), device_id_type=MESH
    )

    def keep(level, node, values):
        return jnp.where(ranks[level, 0, node] > HALF, values, jnp.zeros_like(values))

    def put_node(ref, node, values, level=None):
        ref[node, 0:HALF] = values[0:HALF].astype(BF16)
        low = values[HALF:RANK]
        if level is not None:
            low = keep(level, node, low)
        ref[node, HALF:RANK] = low.astype(BF16)

    def put_pair(ref, first, second, out, level=None):
        put_node(ref, first, out[:RANK], level)
        put_node(ref, second, out[RANK:], level)

    def matrix(level, first, second):
        return jnp.concatenate(
            [
                jnp.concatenate([tiles[level - 1, node, 0], tiles[level - 1, node, 1]], axis=1)
                for node in (first, second)
            ],
            axis=0,
        )

    def two(ref, first, second):
        return jnp.concatenate([ref[first], ref[second]], axis=0)

    def apply(w, x):
        return jnp.dot(w, x, preferred_element_type=F32)

    def apply_t(w, x):
        return lax.dot_general(w, x, (((0,), (0,)), ((), ())), preferred_element_type=F32)

    def copy_f(q, node):
        return pltpu.make_async_remote_copy(
            send_f.at[q], recv_f.at[node], ssem_f.at[q], rsem_f.at[node],
            device_id=(q, blk), device_id_type=MESH,
        )

    def copy_a(q, node):
        return pltpu.make_async_remote_copy(
            send_a.at[q], recv_a.at[node], ssem_a.at[q], rsem_a.at[node],
            device_id=(q, blk), device_id_type=MESH,
        )

    def peer(k):
        return jnp.bitwise_xor(me, k)

    def send(copy, first, last):
        def step(k, carry):
            copy(peer(k), me).start()
            return carry

        lax.fori_loop(max(first, 1), last, step, 0)

    def await_from(copy, first, last):
        def step(k, carry):
            copy(me, peer(k)).wait_recv()
            return carry

        lax.fori_loop(max(first, 1), last, step, 0)

    for c in range(4):
        loads["right"][c].wait()
        for n in range(c * quarter, (c + 1) * quarter):
            put_node(ping, n, apply(basis_in[n], right[n]), 0)
    src, dst = ping, pong
    for level in range(1, MIDDLE):
        tile_loads[level - 1].wait()
        span = 2 ** (level - 1)
        for t in range(PAIRS):
            at = 2 * (t // span) * span + t % span
            out = apply(matrix(level, 2 * t, 2 * t + 1), two(src, at, at + span))
            put_pair(dst, 2 * t, 2 * t + 1, out, level)
        src, dst = dst, src
    tile_loads[MIDDLE - 1].wait()
    pl.semaphore_wait(barrier, NODES - 1 + CHIPS)
    for part_k in (1, 0):
        for k in range(part_k * 8, part_k * 8 + 8):
            h = jnp.bitwise_xor(my_pair, k)
            out = apply(matrix(MIDDLE, 2 * h, 2 * h + 1), two(src, h, h + PAIRS))
            put_pair(send_f, 2 * h, 2 * h + 1, out, MIDDLE)
        send(copy_f, 16 * part_k, 16 * part_k + 16)
    recv_f[me] = send_f[me]

    for c in range(4):
        loads["rows"][c].wait()
        for n in range(c * quarter, (c + 1) * quarter):
            put_node(ping, n, apply(basis_out[n], rows[n]), LEVELS)
    src, dst = ping, pong
    for level in range(LEVELS, MIDDLE + 1, -1):
        tile_loads[level - 1].wait()
        width = 2 ** (LEVELS - level)
        for u in range(PAIRS):
            first = 2 * (u // width) * width + u % width
            out = apply_t(matrix(level, first, first + width), two(src, first, first + width))
            put_pair(dst, 2 * u, 2 * u + 1, out, level - 1)
        src, dst = dst, src
    tile_loads[MIDDLE].wait()
    for part_k in (1, 0):
        for k in range(part_k * 8, part_k * 8 + 8):
            j = jnp.bitwise_xor(my_pair, k)
            out = apply_t(matrix(MIDDLE + 1, j, j + PAIRS), two(src, j, j + PAIRS))
            put_pair(send_a, 2 * j, 2 * j + 1, out)
        send(copy_a, 16 * part_k, 16 * part_k + 16)
    recv_a[me] = send_a[me]

    for level in range(1, MIDDLE + 1):
        span = 2 ** (level - 1)
        for t in range(PAIRS):
            at = 2 * (t // span) * span + t % span
            w = matrix(level, 2 * t, 2 * t + 1)
            if level == MIDDLE:
                w = jnp.concatenate(
                    [
                        w[0:HALF], keep(level, 2 * t, w[HALF:RANK]),
                        w[RANK : RANK + HALF], keep(level, 2 * t + 1, w[RANK + HALF :]),
                    ],
                    axis=0,
                )
            w = w.T
            turned[level - 1, t, 0:HALF] = w[0:HALF]
            turned[level - 1, t, HALF:RANK] = keep(level - 1, at, w[HALF:RANK])
            turned[level - 1, t, RANK : RANK + HALF] = w[RANK : RANK + HALF]
            turned[level - 1, t, RANK + HALF :] = keep(level - 1, at + span, w[RANK + HALF :])

    await_from(copy_f, 0, NODES)
    src, dst = recv_f, ping
    for level in range(MIDDLE + 1, LEVELS + 1):
        width = 2 ** (LEVELS - level)
        for u in range(PAIRS):
            first = 2 * (u // width) * width + u % width
            out = apply(matrix(level, first, first + width), two(src, 2 * u, 2 * u + 1))
            put_pair(dst, first, first + width, out, level)
        src, dst = dst, (pong if dst is ping else ping)

    def swap_copy(y):
        group = 2 * y + 1 - core
        return pltpu.make_async_remote_copy(
            part.at[pl.ds(SHARE * group, SHARE)], swap.at[y], ssem_c.at[y], rsem_c.at[y],
            device_id=(me, chip * 2 + 1 - core), device_id_type=MESH,
        )

    def y_copy(y, slot):
        return pltpu.make_async_remote_copy(
            pair_sum.at[y], gathered.at[slot], ssem_y.at[y], rsem_y.at[slot],
            device_id=(me, 2 * y + core), device_id_type=MESH,
        )

    def row_leaf_out(group):
        for s in range(SHARE):
            n = SHARE * group + s
            part[n] = apply_t(basis_out[n], src[n]).astype(BF16)

    for y in range(CHIPS):
        row_leaf_out(2 * y + 1 - core)
        swap_copy(y).start()
    for y in range(CHIPS):
        row_leaf_out(2 * y + core)

    def add_pair(y):
        swap_copy(y).wait_recv()
        group = 2 * y + core
        for s in range(SHARE):
            pair_sum[y, s] = (
                part[SHARE * group + s].astype(F32) + swap[y, s].astype(F32)
            ).astype(BF16)

    def exchange(k, carry):
        y = lax.rem(chip + k, CHIPS)
        add_pair(y)
        y_copy(y, chip).start()
        return carry

    lax.fori_loop(1, CHIPS, exchange, 0)
    add_pair(chip)

    for part_k in range(4):
        if part_k == 3:
            for k in range(1, CHIPS):
                y = lax.rem(chip + k, CHIPS)
                y_copy(y, y).wait_recv()
            for s in range(SHARE):
                total = pair_sum[chip, s].astype(F32)
                for k in range(1, CHIPS):
                    total = total + gathered[lax.rem(chip + k, CHIPS), s].astype(F32)
                row_out[s] = total.astype(BF16)
        group_k = 3 - part_k
        await_from(copy_a, 8 * group_k, 8 * group_k + 8)
        for k in range(4 * group_k, 4 * group_k + 4):
            h = jnp.bitwise_xor(my_pair, k)
            out = apply(turned[MIDDLE - 1, h], two(recv_a, 2 * h, 2 * h + 1)).astype(BF16)
            ping[h] = out[:RANK]
            ping[h + PAIRS] = out[RANK:]
    src, dst = ping, pong
    for level in range(MIDDLE - 1, 0, -1):
        span = 2 ** (level - 1)
        for t in range(PAIRS):
            at = 2 * (t // span) * span + t % span
            out = apply(turned[level - 1, t], two(src, 2 * t, 2 * t + 1)).astype(BF16)
            dst[at] = out[:RANK]
            dst[at + span] = out[RANK:]
        src, dst = dst, src
    for n in range(NODES):
        col_out[n] = apply_t(basis_in[n], src[n]).astype(BF16)

    def sent(k, carry):
        copy_f(peer(k), me).wait_send()
        copy_a(peer(k), me).wait_send()
        return carry

    lax.fori_loop(1, NODES, sent, 0)
    for y in range(CHIPS):
        swap_copy(y).wait_send()
    for k in range(1, CHIPS):
        y_copy(lax.rem(chip + k, CHIPS), chip).wait_send()


def body(right_sides, row_vectors, leaf_basis_in, leaf_basis_out, transfers, tile_ranks):
    hbm = pl.BlockSpec(memory_space=pl.ANY)
    vmem = pl.BlockSpec(memory_space=pltpu.VMEM)
    nodes = (NODES, RANK, NRHS)
    leaves = (NODES, LEAF, NRHS)
    dma = pltpu.SemaphoreType.DMA
    row, col = pl.pallas_call(
        kernel,
        out_shape=(
            jax.ShapeDtypeStruct((SHARE, LEAF, NRHS), BF16),
            jax.ShapeDtypeStruct(leaves, BF16),
        ),
        in_specs=[hbm, hbm, vmem, vmem, hbm, pl.BlockSpec(memory_space=pltpu.SMEM)],
        out_specs=(vmem, vmem),
        scratch_shapes=[
            pltpu.VMEM(leaves, BF16),
            pltpu.VMEM(leaves, BF16),
            pltpu.VMEM((LEVELS, NODES, 2, RANK, RANK), BF16),
            pltpu.VMEM((MIDDLE, PAIRS, 2 * RANK, 2 * RANK), BF16),
            pltpu.VMEM(nodes, BF16),
            pltpu.VMEM(nodes, BF16),
            pltpu.VMEM(nodes, BF16),
            pltpu.VMEM(nodes, BF16),
            pltpu.VMEM(nodes, BF16),
            pltpu.VMEM(nodes, BF16),
            pltpu.VMEM(leaves, BF16),
            pltpu.VMEM((CHIPS, SHARE, LEAF, NRHS), BF16),
            pltpu.VMEM((CHIPS, SHARE, LEAF, NRHS), BF16),
            pltpu.VMEM((CHIPS, SHARE, LEAF, NRHS), BF16),
            dma((8,)),
            dma((LEVELS,)),
            dma((NODES,)),
            dma((NODES,)),
            dma((NODES,)),
            dma((NODES,)),
            dma((CHIPS,)),
            dma((CHIPS,)),
            dma((CHIPS,)),
            dma((CHIPS,)),
        ],
        compiler_params=pltpu.CompilerParams(
            collective_id=0, has_side_effects=True, vmem_limit_bytes=50 << 20
        ),
        name="butterfly",
    )(
        right_sides.reshape(leaves),
        row_vectors.reshape(leaves),
        jnp.swapaxes(leaf_basis_in[0], 1, 2),
        jnp.swapaxes(leaf_basis_out[0], 1, 2),
        transfers[0],
        jnp.swapaxes(tile_ranks, 0, 1),
    )
    return row.reshape(SHARE * LEAF, NRHS), col.reshape(1, NODES * LEAF, NRHS)


def solution(mesh):
    return jax.shard_map(
        body,
        mesh=mesh,
        in_specs=(
            P("blk", "lvl", None),
            P("lvl", None),
            P("blk", "lvl", None, None),
            P("blk", "lvl", None, None),
            P("blk", None, "lvl", None, None, None),
            P("blk", None, "lvl"),
        ),
        out_specs=(P(("lvl", "blk"), None), P("blk", "lvl", None)),
        check_vma=False,
    )
```

```python
import jax
import jax.numpy as jnp
from jax import lax
from jax.experimental import pallas as pl
from jax.experimental.pallas import tpu as pltpu
from jax.sharding import PartitionSpec as P

LEVELS = 10
MIDDLE = LEVELS // 2
LEAF = 128
RANK = 64
HALF = RANK // 2
NRHS = 256
NODES = 32
PAIRS = NODES // 2
GROUPS = 8
CHIPS = GROUPS // 2
SHARE = NODES // GROUPS
MESH = pl.DeviceIdType.MESH
F32 = jnp.float32
BF16 = jnp.bfloat16


def kernel(
    right_hbm, rows_hbm, basis_in_hbm, basis_out_hbm, tiles_hbm, ranks_hbm,
    row_out, adj_out, basis_in,
    right, rows, basis_out, ranks, tiles, turned, ping, pong, third, fourth,
    send_f, recv_f, send_a, recv_a,
    part, swap, pair_sum, gathered,
    load_sem, basis_sem, tile_sem,
    ssem_f, rsem_f, ssem_a, rsem_a, ssem_c, rsem_c, ssem_y, rsem_y,
):
    me = lax.axis_index("lvl")
    blk = lax.axis_index("blk")
    core = lax.rem(blk, 2)
    chip = blk // 2
    my_pair = me // 2

    quarter = NODES // 4
    loads = {}
    for name, src, dst, base in (("right", right_hbm, right, 0), ("rows", rows_hbm, rows, 4)):
        loads[name] = [
            pltpu.make_async_copy(
                src.at[pl.ds(c * quarter, quarter)],
                dst.at[pl.ds(c * quarter, quarter)],
                load_sem.at[base + c],
            )
            for c in range(4)
        ]
    tile_loads = [
        pltpu.make_async_copy(tiles_hbm.at[l], tiles.at[l], tile_sem.at[l]) for l in range(LEVELS)
    ]
    load_ranks = pltpu.make_async_copy(ranks_hbm, ranks, basis_sem.at[0])
    load_in = pltpu.make_async_copy(basis_in_hbm, basis_in, basis_sem.at[1])
    load_out = pltpu.make_async_copy(basis_out_hbm, basis_out, basis_sem.at[2])
    for copy in [load_ranks, load_in] + loads["right"] + tile_loads[:MIDDLE]:
        copy.start()

    barrier = pltpu.get_barrier_semaphore()

    def greet(k, carry):
        pl.semaphore_signal(
            barrier, inc=1, device_id=(lax.rem(me + k, NODES), blk), device_id_type=MESH
        )
        return carry

    lax.fori_loop(1, NODES, greet, 0)
    for k in range(1, CHIPS):
        other = lax.rem(chip + k, CHIPS) * 2 + core
        pl.semaphore_signal(barrier, inc=1, device_id=(me, other), device_id_type=MESH)
    pl.semaphore_signal(
        barrier, inc=1, device_id=(me, chip * 2 + 1 - core), device_id_type=MESH
    )

    def keep(level, node, values):
        return jnp.where(ranks[level, 0, node] > HALF, values, jnp.zeros_like(values))

    def put_node(ref, node, values, level=None):
        ref[node, 0:HALF] = values[0:HALF].astype(BF16)
        low = values[HALF:RANK]
        if level is not None:
            low = keep(level, node, low)
        ref[node, HALF:RANK] = low.astype(BF16)

    def put_pair(ref, first, second, out, level=None):
        put_node(ref, first, out[:RANK], level)
        put_node(ref, second, out[RANK:], level)

    def matrix(level, first, second):
        return jnp.concatenate(
            [
                jnp.concatenate([tiles[level - 1, node, 0], tiles[level - 1, node, 1]], axis=1)
                for node in (first, second)
            ],
            axis=0,
        )

    def two(ref, first, second):
        return jnp.concatenate([ref[first], ref[second]], axis=0)

    def apply(w, x):
        return jnp.dot(w, x, preferred_element_type=F32)

    def apply_t(w, x):
        return lax.dot_general(w, x, (((0,), (0,)), ((), ())), preferred_element_type=F32)

    def copy_f(q, node):
        return pltpu.make_async_remote_copy(
            send_f.at[q], recv_f.at[node], ssem_f.at[q], rsem_f.at[node],
            device_id=(q, blk), device_id_type=MESH,
        )

    def copy_a(q, node):
        return pltpu.make_async_remote_copy(
            send_a.at[q], recv_a.at[node], ssem_a.at[q], rsem_a.at[node],
            device_id=(q, blk), device_id_type=MESH,
        )

    def peer(k):
        return jnp.bitwise_xor(me, k)

    def send(copy, first, last):
        def step(k, carry):
            copy(peer(k), me).start()
            return carry

        lax.fori_loop(max(first, 1), last, step, 0)

    def await_from(copy, first, last):
        def step(k, carry):
            copy(me, peer(k)).wait_recv()
            return carry

        lax.fori_loop(max(first, 1), last, step, 0)

    load_ranks.wait()
    load_in.wait()
    for c in range(4):
        loads["right"][c].wait()
        for n in range(c * quarter, (c + 1) * quarter):
            put_node(ping, n, apply(basis_in[n], right[n]), 0)
    src, dst = ping, pong
    for level in range(1, MIDDLE):
        tile_loads[level - 1].wait()
        span = 2 ** (level - 1)
        for t in range(PAIRS):
            at = 2 * (t // span) * span + t % span
            out = apply(matrix(level, 2 * t, 2 * t + 1), two(src, at, at + span))
            put_pair(dst, 2 * t, 2 * t + 1, out, level)
        src, dst = dst, src
    tile_loads[MIDDLE - 1].wait()
    for copy in [load_out] + loads["rows"] + tile_loads[: MIDDLE - 1 : -1]:
        copy.start()
    pl.semaphore_wait(barrier, NODES - 1 + CHIPS)
    for part_k in (1, 0):
        for k in range(part_k * 8, part_k * 8 + 8):
            h = jnp.bitwise_xor(my_pair, k)
            out = apply(matrix(MIDDLE, 2 * h, 2 * h + 1), two(src, h, h + PAIRS))
            put_pair(send_f, 2 * h, 2 * h + 1, out, MIDDLE)
        send(copy_f, 16 * part_k, 16 * part_k + 16)
    recv_f[me] = send_f[me]

    load_out.wait()
    for c in range(4):
        loads["rows"][c].wait()
        for n in range(c * quarter, (c + 1) * quarter):
            put_node(ping, n, apply(basis_out[n], rows[n]), LEVELS)
    src, dst = ping, pong
    for level in range(LEVELS, MIDDLE + 1, -1):
        tile_loads[level - 1].wait()
        width = 2 ** (LEVELS - level)
        for u in range(PAIRS):
            first = 2 * (u // width) * width + u % width
            out = apply_t(matrix(level, first, first + width), two(src, first, first + width))
            put_pair(dst, 2 * u, 2 * u + 1, out, level - 1)
        src, dst = dst, src
    tile_loads[MIDDLE].wait()
    for part_k in (1, 0):
        for k in range(part_k * 8, part_k * 8 + 8):
            j = jnp.bitwise_xor(my_pair, k)
            out = apply_t(matrix(MIDDLE + 1, j, j + PAIRS), two(src, j, j + PAIRS))
            put_pair(send_a, 2 * j, 2 * j + 1, out)
    recv_a[me] = send_a[me]

    for level in range(1, MIDDLE + 1):
        span = 2 ** (level - 1)
        for t in range(PAIRS):
            at = 2 * (t // span) * span + t % span
            w = matrix(level, 2 * t, 2 * t + 1)
            if level == MIDDLE:
                w = jnp.concatenate(
                    [
                        w[0:HALF], keep(level, 2 * t, w[HALF:RANK]),
                        w[RANK : RANK + HALF], keep(level, 2 * t + 1, w[RANK + HALF :]),
                    ],
                    axis=0,
                )
            w = w.T
            turned[level - 1, t, 0:HALF] = w[0:HALF]
            turned[level - 1, t, HALF:RANK] = keep(level - 1, at, w[HALF:RANK])
            turned[level - 1, t, RANK : RANK + HALF] = w[RANK : RANK + HALF]
            turned[level - 1, t, RANK + HALF :] = keep(level - 1, at + span, w[RANK + HALF :])

    def left(first, last):
        def step(k, carry):
            copy_f(peer(k), me).wait_send()
            return carry

        lax.fori_loop(max(first, 1), last, step, 0)

    left(16, NODES)
    send(copy_a, 16, NODES)

    await_from(copy_f, 0, NODES)
    src, dst = recv_f, ping
    for level in range(MIDDLE + 1, LEVELS + 1):
        width = 2 ** (LEVELS - level)
        for u in range(PAIRS):
            first = 2 * (u // width) * width + u % width
            out = apply(matrix(level, first, first + width), two(src, 2 * u, 2 * u + 1))
            put_pair(dst, first, first + width, out, level)
        src, dst = dst, (pong if dst is ping else ping)

    def swap_copy(y):
        group = 2 * y + 1 - core
        return pltpu.make_async_remote_copy(
            part.at[pl.ds(SHARE * group, SHARE)], swap.at[y], ssem_c.at[y], rsem_c.at[y],
            device_id=(me, chip * 2 + 1 - core), device_id_type=MESH,
        )

    def y_copy(y, slot):
        return pltpu.make_async_remote_copy(
            pair_sum.at[y], gathered.at[slot], ssem_y.at[y], rsem_y.at[slot],
            device_id=(me, 2 * y + core), device_id_type=MESH,
        )

    def row_leaf_out(group):
        for s in range(SHARE):
            n = SHARE * group + s
            part[n] = apply_t(basis_out[n], src[n]).astype(BF16)

    for y in range(CHIPS):
        row_leaf_out(2 * y + 1 - core)
        swap_copy(y).start()
    for y in range(CHIPS):
        row_leaf_out(2 * y + core)

    def add_pair(y):
        swap_copy(y).wait_recv()
        group = 2 * y + core
        for s in range(SHARE):
            pair_sum[y, s] = (
                part[SHARE * group + s].astype(F32) + swap[y, s].astype(F32)
            ).astype(BF16)

    def exchange(k, carry):
        y = lax.rem(chip + k, CHIPS)
        add_pair(y)
        y_copy(y, chip).start()
        return carry

    lax.fori_loop(1, CHIPS, exchange, 0)
    add_pair(chip)
    left(0, 16)
    send(copy_a, 0, 16)

    def low_t(level, first, last):
        span = 2 ** (level - 1)
        src, dst = steps[MIDDLE - level], steps[MIDDLE + 1 - level]
        for k in range(first, last):
            h = jnp.bitwise_xor(my_pair // (PAIRS // span), k)
            for j in range(PAIRS // span):
                t = j * span + h
                out = apply(turned[level - 1, t], two(src, 2 * t, 2 * t + 1)).astype(BF16)
                at = 2 * j * span + h
                dst[at] = out[:RANK]
                dst[at + span] = out[RANK:]

    steps = (recv_a, ping, pong, third, fourth, adj_out)
    await_from(copy_a, 16, NODES)
    low_t(5, 8, 16)
    low_t(4, 4, 8)
    low_t(3, 2, 4)
    low_t(2, 1, 2)
    await_from(copy_a, 8, 16)
    low_t(5, 4, 8)
    low_t(4, 2, 4)
    low_t(3, 1, 2)
    for k in range(1, CHIPS):
        y = lax.rem(chip + k, CHIPS)
        y_copy(y, y).wait_recv()
    for n in range(SHARE):
        total = pair_sum[chip, n].astype(F32)
        for k in range(1, CHIPS):
            total = total + gathered[lax.rem(chip + k, CHIPS), n].astype(F32)
        row_out[n] = total.astype(BF16)
    await_from(copy_a, 0, 8)
    low_t(5, 0, 4)
    low_t(4, 0, 2)
    low_t(3, 0, 1)
    low_t(2, 0, 1)
    low_t(1, 0, 1)

    def sent(k, carry):
        copy_a(peer(k), me).wait_send()
        return carry

    lax.fori_loop(1, NODES, sent, 0)
    for y in range(CHIPS):
        swap_copy(y).wait_send()
    for k in range(1, CHIPS):
        y_copy(lax.rem(chip + k, CHIPS), chip).wait_send()


def finish(row, adjoint, basis, row_out, col_out, col_buf, store_sem):
    stores = [pltpu.make_async_copy(row, row_out, store_sem.at[4])]
    stores[0].start()
    quarter = NODES // 4
    for c in range(4):
        for n in range(c * quarter, (c + 1) * quarter):
            out = lax.dot_general(
                basis[n], adjoint[n], (((0,), (0,)), ((), ())), preferred_element_type=F32
            )
            col_buf[n] = out.astype(BF16)
        part = pl.ds(c * quarter, quarter)
        stores.append(pltpu.make_async_copy(col_buf.at[part], col_out.at[part], store_sem.at[c]))
        stores[-1].start()
    for copy in stores:
        copy.wait()


def body(right_sides, row_vectors, leaf_basis_in, leaf_basis_out, transfers, tile_ranks):
    hbm = pl.BlockSpec(memory_space=pltpu.HBM)
    vmem = pl.BlockSpec(memory_space=pltpu.VMEM)
    nodes = (NODES, RANK, NRHS)
    leaves = (NODES, LEAF, NRHS)
    dma = pltpu.SemaphoreType.DMA
    row, adjoint, basis = pl.pallas_call(
        kernel,
        out_shape=(
            jax.ShapeDtypeStruct((SHARE, LEAF, NRHS), BF16),
            jax.ShapeDtypeStruct(nodes, BF16),
            jax.ShapeDtypeStruct((NODES, RANK, LEAF), BF16),
        ),
        in_specs=[hbm] * 6,
        out_specs=(vmem, vmem, vmem),
        scratch_shapes=[
            pltpu.VMEM(leaves, BF16),
            pltpu.VMEM(leaves, BF16),
            pltpu.VMEM((NODES, RANK, LEAF), BF16),
            pltpu.SMEM((LEVELS + 1, 1, NODES), jnp.int32),
            pltpu.VMEM((LEVELS, NODES, 2, RANK, RANK), BF16),
            pltpu.VMEM((MIDDLE, PAIRS, 2 * RANK, 2 * RANK), BF16),
            pltpu.VMEM(nodes, BF16),
            pltpu.VMEM(nodes, BF16),
            pltpu.VMEM(nodes, BF16),
            pltpu.VMEM(nodes, BF16),
            pltpu.VMEM(nodes, BF16),
            pltpu.VMEM(nodes, BF16),
            pltpu.VMEM(nodes, BF16),
            pltpu.VMEM(nodes, BF16),
            pltpu.VMEM(leaves, BF16),
            pltpu.VMEM((CHIPS, SHARE, LEAF, NRHS), BF16),
            pltpu.VMEM((CHIPS, SHARE, LEAF, NRHS), BF16),
            pltpu.VMEM((CHIPS, SHARE, LEAF, NRHS), BF16),
            dma((8,)),
            dma((3,)),
            dma((LEVELS,)),
            dma((NODES,)),
            dma((NODES,)),
            dma((NODES,)),
            dma((NODES,)),
            dma((CHIPS,)),
            dma((CHIPS,)),
            dma((CHIPS,)),
            dma((CHIPS,)),
        ],
        compiler_params=pltpu.CompilerParams(
            collective_id=0, has_side_effects=True, vmem_limit_bytes=50 << 20
        ),
        name="butterfly",
    )(
        *(
            pltpu.with_memory_space_constraint(array, pltpu.HBM)
            for array in (
                right_sides.reshape(leaves),
                row_vectors.reshape(leaves),
                jnp.swapaxes(leaf_basis_in[0], 1, 2),
                jnp.swapaxes(leaf_basis_out[0], 1, 2),
                transfers[0],
                jnp.swapaxes(tile_ranks, 0, 1),
            )
        )
    )
    row, col = pl.pallas_call(
        finish,
        out_shape=(
            jax.ShapeDtypeStruct((SHARE, LEAF, NRHS), BF16),
            jax.ShapeDtypeStruct(leaves, BF16),
        ),
        in_specs=[vmem, vmem, vmem],
        out_specs=(hbm, hbm),
        scratch_shapes=[pltpu.VMEM(leaves, BF16), dma((5,))],
        compiler_params=pltpu.CompilerParams(vmem_limit_bytes=50 << 20),
        name="leaves_out",
    )(row, adjoint, basis)
    return row.reshape(SHARE * LEAF, NRHS), col.reshape(1, NODES * LEAF, NRHS)


def solution(mesh):
    return jax.shard_map(
        body,
        mesh=mesh,
        in_specs=(
            P("blk", "lvl", None),
            P("lvl", None),
            P("blk", "lvl", None, None),
            P("blk", "lvl", None, None),
            P("blk", None, "lvl", None, None, None),
            P("blk", None, "lvl"),
        ),
        out_specs=(P(("lvl", "blk"), None), P("blk", "lvl", None)),
        check_vma=False,
    )
```

```python
import jax
import jax.numpy as jnp
from jax import lax
from jax.experimental import pallas as pl
from jax.experimental.pallas import tpu as pltpu
from jax.sharding import PartitionSpec as P

LEVELS = 10
MIDDLE = LEVELS // 2
LEAF = 128
RANK = 64
HALF = RANK // 2
NRHS = 256
NODES = 32
PAIRS = NODES // 2
GROUPS = 8
CHIPS = GROUPS // 2
SHARE = NODES // GROUPS
FAR = (4, 3, 5, 2)
NEAR = (6, 1, 7, 0)
MESH = pl.DeviceIdType.MESH
F32 = jnp.float32
BF16 = jnp.bfloat16


def kernel(
    right_hbm, rows_hbm, basis_in_hbm, basis_out_hbm, tiles_hbm, ranks_hbm,
    row_out, adj_out, basis_in,
    right, rows, basis_out, ranks, tiles, turned, ping, pong, third, fourth,
    send_f, recv_f, send_a, recv_a,
    part, swap, pair_sum, gathered,
    load_sem, basis_sem, tile_sem,
    ssem_f, rsem_f, ssem_a, rsem_a, ssem_c, rsem_c, ssem_y, rsem_y,
):
    me = lax.axis_index("lvl")
    blk = lax.axis_index("blk")
    core = lax.rem(blk, 2)
    chip = blk // 2
    my_pair = me // 2

    quarter = NODES // 4
    loads = {}
    for name, src, dst, base in (("right", right_hbm, right, 0), ("rows", rows_hbm, rows, 4)):
        loads[name] = [
            pltpu.make_async_copy(
                src.at[pl.ds(c * quarter, quarter)],
                dst.at[pl.ds(c * quarter, quarter)],
                load_sem.at[base + c],
            )
            for c in range(4)
        ]
    tile_loads = [
        pltpu.make_async_copy(tiles_hbm.at[l], tiles.at[l], tile_sem.at[l]) for l in range(LEVELS)
    ]
    load_ranks = pltpu.make_async_copy(ranks_hbm, ranks, basis_sem.at[0])
    load_in = pltpu.make_async_copy(basis_in_hbm, basis_in, basis_sem.at[1])
    load_out = pltpu.make_async_copy(basis_out_hbm, basis_out, basis_sem.at[2])
    for copy in [load_ranks, load_in] + loads["right"] + tile_loads[:MIDDLE]:
        copy.start()

    barrier = pltpu.get_barrier_semaphore()

    def greet(k, carry):
        pl.semaphore_signal(
            barrier, inc=1, device_id=(lax.rem(me + k, NODES), blk), device_id_type=MESH
        )
        return carry

    lax.fori_loop(1, NODES, greet, 0)
    for k in range(1, CHIPS):
        other = lax.rem(chip + k, CHIPS) * 2 + core
        pl.semaphore_signal(barrier, inc=1, device_id=(me, other), device_id_type=MESH)
    pl.semaphore_signal(
        barrier, inc=1, device_id=(me, chip * 2 + 1 - core), device_id_type=MESH
    )

    def keep(level, node, values):
        return jnp.where(ranks[level, 0, node] > HALF, values, jnp.zeros_like(values))

    def put_node(ref, node, values, level=None):
        ref[node, 0:HALF] = values[0:HALF].astype(BF16)
        low = values[HALF:RANK]
        if level is not None:
            low = keep(level, node, low)
        ref[node, HALF:RANK] = low.astype(BF16)

    def put_pair(ref, first, second, out, level=None):
        put_node(ref, first, out[:RANK], level)
        put_node(ref, second, out[RANK:], level)

    def matrix(level, first, second):
        return jnp.concatenate(
            [
                jnp.concatenate([tiles[level - 1, node, 0], tiles[level - 1, node, 1]], axis=1)
                for node in (first, second)
            ],
            axis=0,
        )

    def two(ref, first, second):
        return jnp.concatenate([ref[first], ref[second]], axis=0)

    def apply(w, x):
        return jnp.dot(w, x, preferred_element_type=F32)

    def apply_t(w, x):
        return lax.dot_general(w, x, (((0,), (0,)), ((), ())), preferred_element_type=F32)

    def copy_f(q, node):
        return pltpu.make_async_remote_copy(
            send_f.at[q], recv_f.at[node], ssem_f.at[q], rsem_f.at[node],
            device_id=(q, blk), device_id_type=MESH,
        )

    def copy_a(q, node):
        return pltpu.make_async_remote_copy(
            send_a.at[q], recv_a.at[node], ssem_a.at[q], rsem_a.at[node],
            device_id=(q, blk), device_id_type=MESH,
        )

    def peer(k):
        return jnp.bitwise_xor(me, k)

    def each(shifts, act):
        for dz in shifts:

            def step(dx, carry, dz=dz):
                act(lax.rem(me // 4 + dz, 8) * 4 + lax.rem(me + dx, 4))
                return carry

            lax.fori_loop(0 if dz else 1, 4, step, 0)

    def send(copy, shifts):
        each(shifts, lambda q: copy(q, me).start())

    def await_from(copy, first, last):
        def step(k, carry):
            copy(me, peer(k)).wait_recv()
            return carry

        lax.fori_loop(max(first, 1), last, step, 0)

    load_ranks.wait()
    load_in.wait()
    for c in range(4):
        loads["right"][c].wait()
        for n in range(c * quarter, (c + 1) * quarter):
            put_node(ping, n, apply(basis_in[n], right[n]), 0)
    src, dst = ping, pong
    for level in range(1, MIDDLE):
        tile_loads[level - 1].wait()
        span = 2 ** (level - 1)
        for t in range(PAIRS):
            at = 2 * (t // span) * span + t % span
            out = apply(matrix(level, 2 * t, 2 * t + 1), two(src, at, at + span))
            put_pair(dst, 2 * t, 2 * t + 1, out, level)
        src, dst = dst, src
    tile_loads[MIDDLE - 1].wait()
    for copy in [load_out] + loads["rows"] + tile_loads[: MIDDLE - 1 : -1]:
        copy.start()
    for h in range(PAIRS):
        out = apply(matrix(MIDDLE, 2 * h, 2 * h + 1), two(src, h, h + PAIRS))
        put_pair(send_f, 2 * h, 2 * h + 1, out, MIDDLE)
    pl.semaphore_wait(barrier, NODES - 1 + CHIPS)
    send(copy_f, FAR + NEAR)
    recv_f[me] = send_f[me]

    load_out.wait()
    for c in range(4):
        loads["rows"][c].wait()
        for n in range(c * quarter, (c + 1) * quarter):
            put_node(ping, n, apply(basis_out[n], rows[n]), LEVELS)
    src, dst = ping, pong
    for level in range(LEVELS, MIDDLE + 1, -1):
        tile_loads[level - 1].wait()
        width = 2 ** (LEVELS - level)
        for u in range(PAIRS):
            first = 2 * (u // width) * width + u % width
            out = apply_t(matrix(level, first, first + width), two(src, first, first + width))
            put_pair(dst, 2 * u, 2 * u + 1, out, level - 1)
        src, dst = dst, src
    tile_loads[MIDDLE].wait()
    for j in range(PAIRS):
        out = apply_t(matrix(MIDDLE + 1, j, j + PAIRS), two(src, j, j + PAIRS))
        put_pair(send_a, 2 * j, 2 * j + 1, out)
    recv_a[me] = send_a[me]

    for level in range(1, MIDDLE + 1):
        span = 2 ** (level - 1)
        for t in range(PAIRS):
            at = 2 * (t // span) * span + t % span
            w = matrix(level, 2 * t, 2 * t + 1)
            if level == MIDDLE:
                w = jnp.concatenate(
                    [
                        w[0:HALF], keep(level, 2 * t, w[HALF:RANK]),
                        w[RANK : RANK + HALF], keep(level, 2 * t + 1, w[RANK + HALF :]),
                    ],
                    axis=0,
                )
            w = w.T
            turned[level - 1, t, 0:HALF] = w[0:HALF]
            turned[level - 1, t, HALF:RANK] = keep(level - 1, at, w[HALF:RANK])
            turned[level - 1, t, RANK : RANK + HALF] = w[RANK : RANK + HALF]
            turned[level - 1, t, RANK + HALF :] = keep(level - 1, at + span, w[RANK + HALF :])

    def left(shifts):
        each(shifts, lambda q: copy_f(q, me).wait_send())

    left(FAR)
    send(copy_a, FAR)

    await_from(copy_f, 0, NODES)
    src, dst = recv_f, ping
    for level in range(MIDDLE + 1, LEVELS + 1):
        width = 2 ** (LEVELS - level)
        for u in range(PAIRS):
            first = 2 * (u // width) * width + u % width
            out = apply(matrix(level, first, first + width), two(src, 2 * u, 2 * u + 1))
            put_pair(dst, first, first + width, out, level)
        src, dst = dst, (pong if dst is ping else ping)

    def swap_copy(y):
        group = 2 * y + 1 - core
        return pltpu.make_async_remote_copy(
            part.at[pl.ds(SHARE * group, SHARE)], swap.at[y], ssem_c.at[y], rsem_c.at[y],
            device_id=(me, chip * 2 + 1 - core), device_id_type=MESH,
        )

    def y_copy(y, slot):
        return pltpu.make_async_remote_copy(
            pair_sum.at[y], gathered.at[slot], ssem_y.at[y], rsem_y.at[slot],
            device_id=(me, 2 * y + core), device_id_type=MESH,
        )

    def row_leaf_out(group):
        for s in range(SHARE):
            n = SHARE * group + s
            part[n] = apply_t(basis_out[n], src[n]).astype(BF16)

    for y in range(CHIPS):
        row_leaf_out(2 * y + 1 - core)
        swap_copy(y).start()
    for y in range(CHIPS):
        row_leaf_out(2 * y + core)

    def add_pair(y):
        swap_copy(y).wait_recv()
        group = 2 * y + core
        for s in range(SHARE):
            pair_sum[y, s] = (
                part[SHARE * group + s].astype(F32) + swap[y, s].astype(F32)
            ).astype(BF16)

    def exchange(k, carry):
        y = lax.rem(chip + k, CHIPS)
        add_pair(y)
        y_copy(y, chip).start()
        return carry

    lax.fori_loop(1, CHIPS, exchange, 0)
    add_pair(chip)
    left(NEAR)
    send(copy_a, NEAR)

    def low_t(level, first, last):
        span = 2 ** (level - 1)
        src, dst = steps[MIDDLE - level], steps[MIDDLE + 1 - level]
        for k in range(first, last):
            h = jnp.bitwise_xor(my_pair // (PAIRS // span), k)
            for j in range(PAIRS // span):
                t = j * span + h
                out = apply(turned[level - 1, t], two(src, 2 * t, 2 * t + 1)).astype(BF16)
                at = 2 * j * span + h
                dst[at] = out[:RANK]
                dst[at + span] = out[RANK:]

    steps = (recv_a, ping, pong, third, fourth, adj_out)
    await_from(copy_a, 16, NODES)
    low_t(5, 8, 16)
    low_t(4, 4, 8)
    low_t(3, 2, 4)
    low_t(2, 1, 2)
    await_from(copy_a, 8, 16)
    low_t(5, 4, 8)
    low_t(4, 2, 4)
    low_t(3, 1, 2)
    await_from(copy_a, 0, 8)
    low_t(5, 0, 4)
    low_t(4, 0, 2)
    low_t(3, 0, 1)
    low_t(2, 0, 1)
    low_t(1, 0, 1)
    for k in range(1, CHIPS):
        y = lax.rem(chip + k, CHIPS)
        y_copy(y, y).wait_recv()
    for n in range(SHARE):
        total = pair_sum[chip, n].astype(F32)
        for k in range(1, CHIPS):
            total = total + gathered[lax.rem(chip + k, CHIPS), n].astype(F32)
        row_out[n] = total.astype(BF16)

    def sent(k, carry):
        copy_a(peer(k), me).wait_send()
        return carry

    lax.fori_loop(1, NODES, sent, 0)
    for y in range(CHIPS):
        swap_copy(y).wait_send()
    for k in range(1, CHIPS):
        y_copy(lax.rem(chip + k, CHIPS), chip).wait_send()


def finish(row, adjoint, basis, row_out, col_out, col_buf, store_sem):
    stores = [pltpu.make_async_copy(row, row_out, store_sem.at[4])]
    stores[0].start()
    quarter = NODES // 4
    for c in range(4):
        for n in range(c * quarter, (c + 1) * quarter):
            out = lax.dot_general(
                basis[n], adjoint[n], (((0,), (0,)), ((), ())), preferred_element_type=F32
            )
            col_buf[n] = out.astype(BF16)
        part = pl.ds(c * quarter, quarter)
        stores.append(pltpu.make_async_copy(col_buf.at[part], col_out.at[part], store_sem.at[c]))
        stores[-1].start()
    for copy in stores:
        copy.wait()


def body(right_sides, row_vectors, leaf_basis_in, leaf_basis_out, transfers, tile_ranks):
    hbm = pl.BlockSpec(memory_space=pltpu.HBM)
    vmem = pl.BlockSpec(memory_space=pltpu.VMEM)
    nodes = (NODES, RANK, NRHS)
    leaves = (NODES, LEAF, NRHS)
    dma = pltpu.SemaphoreType.DMA
    row, adjoint, basis = pl.pallas_call(
        kernel,
        out_shape=(
            jax.ShapeDtypeStruct((SHARE, LEAF, NRHS), BF16),
            jax.ShapeDtypeStruct(nodes, BF16),
            jax.ShapeDtypeStruct((NODES, RANK, LEAF), BF16),
        ),
        in_specs=[hbm] * 6,
        out_specs=(vmem, vmem, vmem),
        scratch_shapes=[
            pltpu.VMEM(leaves, BF16),
            pltpu.VMEM(leaves, BF16),
            pltpu.VMEM((NODES, RANK, LEAF), BF16),
            pltpu.SMEM((LEVELS + 1, 1, NODES), jnp.int32),
            pltpu.VMEM((LEVELS, NODES, 2, RANK, RANK), BF16),
            pltpu.VMEM((MIDDLE, PAIRS, 2 * RANK, 2 * RANK), BF16),
            pltpu.VMEM(nodes, BF16),
            pltpu.VMEM(nodes, BF16),
            pltpu.VMEM(nodes, BF16),
            pltpu.VMEM(nodes, BF16),
            pltpu.VMEM(nodes, BF16),
            pltpu.VMEM(nodes, BF16),
            pltpu.VMEM(nodes, BF16),
            pltpu.VMEM(nodes, BF16),
            pltpu.VMEM(leaves, BF16),
            pltpu.VMEM((CHIPS, SHARE, LEAF, NRHS), BF16),
            pltpu.VMEM((CHIPS, SHARE, LEAF, NRHS), BF16),
            pltpu.VMEM((CHIPS, SHARE, LEAF, NRHS), BF16),
            dma((8,)),
            dma((3,)),
            dma((LEVELS,)),
            dma((NODES,)),
            dma((NODES,)),
            dma((NODES,)),
            dma((NODES,)),
            dma((CHIPS,)),
            dma((CHIPS,)),
            dma((CHIPS,)),
            dma((CHIPS,)),
        ],
        compiler_params=pltpu.CompilerParams(
            collective_id=0, has_side_effects=True, vmem_limit_bytes=50 << 20
        ),
        name="butterfly",
    )(
        *(
            pltpu.with_memory_space_constraint(array, pltpu.HBM)
            for array in (
                right_sides.reshape(leaves),
                row_vectors.reshape(leaves),
                jnp.swapaxes(leaf_basis_in[0], 1, 2),
                jnp.swapaxes(leaf_basis_out[0], 1, 2),
                transfers[0],
                jnp.swapaxes(tile_ranks, 0, 1),
            )
        )
    )
    row, col = pl.pallas_call(
        finish,
        out_shape=(
            jax.ShapeDtypeStruct((SHARE, LEAF, NRHS), BF16),
            jax.ShapeDtypeStruct(leaves, BF16),
        ),
        in_specs=[vmem, vmem, vmem],
        out_specs=(hbm, hbm),
        scratch_shapes=[pltpu.VMEM(leaves, BF16), dma((5,))],
        compiler_params=pltpu.CompilerParams(vmem_limit_bytes=50 << 20),
        name="leaves_out",
    )(row, adjoint, basis)
    return row.reshape(SHARE * LEAF, NRHS), col.reshape(1, NODES * LEAF, NRHS)


def solution(mesh):
    return jax.shard_map(
        body,
        mesh=mesh,
        in_specs=(
            P("blk", "lvl", None),
            P("lvl", None),
            P("blk", "lvl", None, None),
            P("blk", "lvl", None, None),
            P("blk", None, "lvl", None, None, None),
            P("blk", None, "lvl"),
        ),
        out_specs=(P(("lvl", "blk"), None), P("blk", "lvl", None)),
        check_vma=False,
    )
```

```python
import jax
import jax.numpy as jnp
from jax import lax
from jax.experimental import pallas as pl
from jax.experimental.pallas import tpu as pltpu
from jax.sharding import PartitionSpec as P

LEVELS = 10
MIDDLE = LEVELS // 2
LEAF = 128
RANK = 64
HALF = RANK // 2
NRHS = 256
NODES = 32
PAIRS = NODES // 2
GROUPS = 8
CHIPS = GROUPS // 2
SHARE = NODES // GROUPS
FAR = (4, 3, 5, 2)
NEAR = (6, 1, 7, 0)
MESH = pl.DeviceIdType.MESH
F32 = jnp.float32
BF16 = jnp.bfloat16


def kernel(
    right_hbm, rows_hbm, basis_in_hbm, basis_out_hbm, tiles_hbm, ranks_hbm,
    row_out, adj_out, basis_in,
    right, rows, basis_out, ranks, tiles, turned, ping, pong, third, fourth,
    send_f, recv_f, send_a, recv_a,
    part, swap, pair_sum, gathered,
    load_sem, basis_sem, tile_sem,
    ssem_f, rsem_f, ssem_a, rsem_a, ssem_c, rsem_c, ssem_y, rsem_y,
):
    me = lax.axis_index("lvl")
    blk = lax.axis_index("blk")
    core = lax.rem(blk, 2)
    chip = blk // 2
    my_pair = me // 2

    quarter = NODES // 4
    loads = {}
    for name, src, dst, base in (("right", right_hbm, right, 0), ("rows", rows_hbm, rows, 4)):
        loads[name] = [
            pltpu.make_async_copy(
                src.at[pl.ds(c * quarter, quarter)],
                dst.at[pl.ds(c * quarter, quarter)],
                load_sem.at[base + c],
            )
            for c in range(4)
        ]
    tile_loads = [
        pltpu.make_async_copy(tiles_hbm.at[l], tiles.at[l], tile_sem.at[l]) for l in range(LEVELS)
    ]
    load_ranks = pltpu.make_async_copy(ranks_hbm, ranks, basis_sem.at[0])
    load_in = pltpu.make_async_copy(basis_in_hbm, basis_in, basis_sem.at[1])
    load_out = pltpu.make_async_copy(basis_out_hbm, basis_out, basis_sem.at[2])
    for copy in [load_ranks, load_in] + loads["right"] + tile_loads[:MIDDLE]:
        copy.start()

    barrier = pltpu.get_barrier_semaphore()

    for dz in FAR + NEAR:

        def greet(dx, carry, dz=dz):
            peer_z = lax.rem(me // 4 + dz, 8) * 4 + lax.rem(me + dx, 4)
            pl.semaphore_signal(barrier, inc=1, device_id=(peer_z, blk), device_id_type=MESH)
            return carry

        lax.fori_loop(0 if dz else 1, 4, greet, 0)
    for k in range(1, CHIPS):
        other = lax.rem(chip + k, CHIPS) * 2 + core
        pl.semaphore_signal(barrier, inc=1, device_id=(me, other), device_id_type=MESH)
    pl.semaphore_signal(
        barrier, inc=1, device_id=(me, chip * 2 + 1 - core), device_id_type=MESH
    )

    def keep(level, node, values):
        return jnp.where(ranks[level, 0, node] > HALF, values, jnp.zeros_like(values))

    def put_node(ref, node, values, level=None):
        ref[node, 0:HALF] = values[0:HALF].astype(BF16)
        low = values[HALF:RANK]
        if level is not None:
            low = keep(level, node, low)
        ref[node, HALF:RANK] = low.astype(BF16)

    def put_pair(ref, first, second, out, level=None):
        put_node(ref, first, out[:RANK], level)
        put_node(ref, second, out[RANK:], level)

    def matrix(level, first, second):
        return jnp.concatenate(
            [
                jnp.concatenate([tiles[level - 1, node, 0], tiles[level - 1, node, 1]], axis=1)
                for node in (first, second)
            ],
            axis=0,
        )

    def two(ref, first, second):
        return jnp.concatenate([ref[first], ref[second]], axis=0)

    def apply(w, x):
        return jnp.dot(w, x, preferred_element_type=F32)

    def apply_t(w, x):
        return lax.dot_general(w, x, (((0,), (0,)), ((), ())), preferred_element_type=F32)

    def copy_f(q, node):
        return pltpu.make_async_remote_copy(
            send_f.at[q], recv_f.at[node], ssem_f.at[q], rsem_f.at[node],
            device_id=(q, blk), device_id_type=MESH,
        )

    def copy_a(q, node):
        return pltpu.make_async_remote_copy(
            send_a.at[q], recv_a.at[node], ssem_a.at[q], rsem_a.at[node],
            device_id=(q, blk), device_id_type=MESH,
        )

    def peer(k):
        return jnp.bitwise_xor(me, k)

    def each(shifts, act):
        for dz in shifts:

            def step(dx, carry, dz=dz):
                act(lax.rem(me // 4 + dz, 8) * 4 + lax.rem(me + dx, 4))
                return carry

            lax.fori_loop(0 if dz else 1, 4, step, 0)

    def send(copy, shifts):
        each(shifts, lambda q: copy(q, me).start())

    def await_from(copy, first, last):
        def step(k, carry):
            copy(me, peer(k)).wait_recv()
            return carry

        lax.fori_loop(max(first, 1), last, step, 0)

    load_ranks.wait()
    load_in.wait()
    for c in range(4):
        loads["right"][c].wait()
        for n in range(c * quarter, (c + 1) * quarter):
            put_node(ping, n, apply(basis_in[n], right[n]), 0)
    src, dst = ping, pong
    for level in range(1, MIDDLE):
        tile_loads[level - 1].wait()
        span = 2 ** (level - 1)
        for t in range(PAIRS):
            at = 2 * (t // span) * span + t % span
            out = apply(matrix(level, 2 * t, 2 * t + 1), two(src, at, at + span))
            put_pair(dst, 2 * t, 2 * t + 1, out, level)
        src, dst = dst, src
    tile_loads[MIDDLE - 1].wait()
    for copy in [load_out] + loads["rows"] + tile_loads[: MIDDLE - 1 : -1]:
        copy.start()
    for h in range(PAIRS):
        out = apply(matrix(MIDDLE, 2 * h, 2 * h + 1), two(src, h, h + PAIRS))
        put_pair(send_f, 2 * h, 2 * h + 1, out, MIDDLE)
    pl.semaphore_wait(barrier, NODES - 1 + CHIPS)
    send(copy_f, FAR + NEAR)
    recv_f[me] = send_f[me]

    load_out.wait()
    for c in range(4):
        loads["rows"][c].wait()
        for n in range(c * quarter, (c + 1) * quarter):
            put_node(ping, n, apply(basis_out[n], rows[n]), LEVELS)
    src, dst = ping, pong
    for level in range(LEVELS, MIDDLE + 1, -1):
        tile_loads[level - 1].wait()
        width = 2 ** (LEVELS - level)
        for u in range(PAIRS):
            first = 2 * (u // width) * width + u % width
            out = apply_t(matrix(level, first, first + width), two(src, first, first + width))
            put_pair(dst, 2 * u, 2 * u + 1, out, level - 1)
        src, dst = dst, src
    tile_loads[MIDDLE].wait()
    for j in range(PAIRS):
        out = apply_t(matrix(MIDDLE + 1, j, j + PAIRS), two(src, j, j + PAIRS))
        put_pair(send_a, 2 * j, 2 * j + 1, out)
    recv_a[me] = send_a[me]

    for level in range(1, MIDDLE + 1):
        span = 2 ** (level - 1)
        for t in range(PAIRS):
            at = 2 * (t // span) * span + t % span
            w = matrix(level, 2 * t, 2 * t + 1)
            if level == MIDDLE:
                w = jnp.concatenate(
                    [
                        w[0:HALF], keep(level, 2 * t, w[HALF:RANK]),
                        w[RANK : RANK + HALF], keep(level, 2 * t + 1, w[RANK + HALF :]),
                    ],
                    axis=0,
                )
            w = w.T
            turned[level - 1, t, 0:HALF] = w[0:HALF]
            turned[level - 1, t, HALF:RANK] = keep(level - 1, at, w[HALF:RANK])
            turned[level - 1, t, RANK : RANK + HALF] = w[RANK : RANK + HALF]
            turned[level - 1, t, RANK + HALF :] = keep(level - 1, at + span, w[RANK + HALF :])

    def left(shifts):
        each(shifts, lambda q: copy_f(q, me).wait_send())

    left(FAR)
    send(copy_a, FAR)

    await_from(copy_f, 0, NODES)
    src, dst = recv_f, ping
    for level in range(MIDDLE + 1, LEVELS + 1):
        width = 2 ** (LEVELS - level)
        for u in range(PAIRS):
            first = 2 * (u // width) * width + u % width
            out = apply(matrix(level, first, first + width), two(src, 2 * u, 2 * u + 1))
            put_pair(dst, first, first + width, out, level)
        src, dst = dst, (pong if dst is ping else ping)

    def swap_copy(y):
        group = 2 * y + 1 - core
        return pltpu.make_async_remote_copy(
            part.at[pl.ds(SHARE * group, SHARE)], swap.at[y], ssem_c.at[y], rsem_c.at[y],
            device_id=(me, chip * 2 + 1 - core), device_id_type=MESH,
        )

    def y_copy(y, slot):
        return pltpu.make_async_remote_copy(
            pair_sum.at[y], gathered.at[slot], ssem_y.at[y], rsem_y.at[slot],
            device_id=(me, 2 * y + core), device_id_type=MESH,
        )

    def row_leaf_out(group):
        for s in range(SHARE):
            n = SHARE * group + s
            part[n] = apply_t(basis_out[n], src[n]).astype(BF16)

    for y in range(CHIPS):
        row_leaf_out(2 * y + 1 - core)
        swap_copy(y).start()
    for y in range(CHIPS):
        row_leaf_out(2 * y + core)

    def add_pair(y):
        swap_copy(y).wait_recv()
        group = 2 * y + core
        for s in range(SHARE):
            pair_sum[y, s] = (
                part[SHARE * group + s].astype(F32) + swap[y, s].astype(F32)
            ).astype(BF16)

    def exchange(k, carry):
        y = lax.rem(chip + k, CHIPS)
        add_pair(y)
        y_copy(y, chip).start()
        return carry

    lax.fori_loop(1, CHIPS, exchange, 0)
    add_pair(chip)
    left(NEAR)
    send(copy_a, NEAR)

    def low_t(level, first, last):
        span = 2 ** (level - 1)
        src, dst = steps[MIDDLE - level], steps[MIDDLE + 1 - level]
        for k in range(first, last):
            h = jnp.bitwise_xor(my_pair // (PAIRS // span), k)
            for j in range(PAIRS // span):
                t = j * span + h
                out = apply(turned[level - 1, t], two(src, 2 * t, 2 * t + 1)).astype(BF16)
                at = 2 * j * span + h
                dst[at] = out[:RANK]
                dst[at + span] = out[RANK:]

    steps = (recv_a, ping, pong, third, fourth, adj_out)
    await_from(copy_a, 16, NODES)
    low_t(5, 8, 16)
    low_t(4, 4, 8)
    low_t(3, 2, 4)
    low_t(2, 1, 2)
    await_from(copy_a, 8, 16)
    low_t(5, 4, 8)
    low_t(4, 2, 4)
    low_t(3, 1, 2)
    await_from(copy_a, 0, 8)
    low_t(5, 0, 4)
    low_t(4, 0, 2)
    low_t(3, 0, 1)
    low_t(2, 0, 1)
    low_t(1, 0, 1)
    for k in range(1, CHIPS):
        y = lax.rem(chip + k, CHIPS)
        y_copy(y, y).wait_recv()
    for n in range(SHARE):
        total = pair_sum[chip, n].astype(F32)
        for k in range(1, CHIPS):
            total = total + gathered[lax.rem(chip + k, CHIPS), n].astype(F32)
        row_out[n] = total.astype(BF16)

    def sent(k, carry):
        copy_a(peer(k), me).wait_send()
        return carry

    lax.fori_loop(1, NODES, sent, 0)
    for y in range(CHIPS):
        swap_copy(y).wait_send()
    for k in range(1, CHIPS):
        y_copy(lax.rem(chip + k, CHIPS), chip).wait_send()


def finish(row, adjoint, basis, row_out, col_out, col_buf, store_sem):
    stores = [pltpu.make_async_copy(row, row_out, store_sem.at[4])]
    stores[0].start()
    quarter = NODES // 4
    for c in range(4):
        for n in range(c * quarter, (c + 1) * quarter):
            out = lax.dot_general(
                basis[n], adjoint[n], (((0,), (0,)), ((), ())), preferred_element_type=F32
            )
            col_buf[n] = out.astype(BF16)
        part = pl.ds(c * quarter, quarter)
        stores.append(pltpu.make_async_copy(col_buf.at[part], col_out.at[part], store_sem.at[c]))
        stores[-1].start()
    for copy in stores:
        copy.wait()


def body(right_sides, row_vectors, leaf_basis_in, leaf_basis_out, transfers, tile_ranks):
    hbm = pl.BlockSpec(memory_space=pltpu.HBM)
    vmem = pl.BlockSpec(memory_space=pltpu.VMEM)
    nodes = (NODES, RANK, NRHS)
    leaves = (NODES, LEAF, NRHS)
    dma = pltpu.SemaphoreType.DMA
    row, adjoint, basis = pl.pallas_call(
        kernel,
        out_shape=(
            jax.ShapeDtypeStruct((SHARE, LEAF, NRHS), BF16),
            jax.ShapeDtypeStruct(nodes, BF16),
            jax.ShapeDtypeStruct((NODES, RANK, LEAF), BF16),
        ),
        in_specs=[hbm] * 6,
        out_specs=(vmem, vmem, vmem),
        scratch_shapes=[
            pltpu.VMEM(leaves, BF16),
            pltpu.VMEM(leaves, BF16),
            pltpu.VMEM((NODES, RANK, LEAF), BF16),
            pltpu.SMEM((LEVELS + 1, 1, NODES), jnp.int32),
            pltpu.VMEM((LEVELS, NODES, 2, RANK, RANK), BF16),
            pltpu.VMEM((MIDDLE, PAIRS, 2 * RANK, 2 * RANK), BF16),
            pltpu.VMEM(nodes, BF16),
            pltpu.VMEM(nodes, BF16),
            pltpu.VMEM(nodes, BF16),
            pltpu.VMEM(nodes, BF16),
            pltpu.VMEM(nodes, BF16),
            pltpu.VMEM(nodes, BF16),
            pltpu.VMEM(nodes, BF16),
            pltpu.VMEM(nodes, BF16),
            pltpu.VMEM(leaves, BF16),
            pltpu.VMEM((CHIPS, SHARE, LEAF, NRHS), BF16),
            pltpu.VMEM((CHIPS, SHARE, LEAF, NRHS), BF16),
            pltpu.VMEM((CHIPS, SHARE, LEAF, NRHS), BF16),
            dma((8,)),
            dma((3,)),
            dma((LEVELS,)),
            dma((NODES,)),
            dma((NODES,)),
            dma((NODES,)),
            dma((NODES,)),
            dma((CHIPS,)),
            dma((CHIPS,)),
            dma((CHIPS,)),
            dma((CHIPS,)),
        ],
        compiler_params=pltpu.CompilerParams(
            collective_id=0, has_side_effects=True, vmem_limit_bytes=50 << 20
        ),
        name="butterfly",
    )(
        *(
            pltpu.with_memory_space_constraint(array, pltpu.HBM)
            for array in (
                right_sides.reshape(leaves),
                row_vectors.reshape(leaves),
                jnp.swapaxes(leaf_basis_in[0], 1, 2),
                jnp.swapaxes(leaf_basis_out[0], 1, 2),
                transfers[0],
                jnp.swapaxes(tile_ranks, 0, 1),
            )
        )
    )
    row, col = pl.pallas_call(
        finish,
        out_shape=(
            jax.ShapeDtypeStruct((SHARE, LEAF, NRHS), BF16),
            jax.ShapeDtypeStruct(leaves, BF16),
        ),
        in_specs=[vmem, vmem, vmem],
        out_specs=(hbm, hbm),
        scratch_shapes=[pltpu.VMEM(leaves, BF16), dma((5,))],
        compiler_params=pltpu.CompilerParams(vmem_limit_bytes=50 << 20),
        name="leaves_out",
    )(row, adjoint, basis)
    return row.reshape(SHARE * LEAF, NRHS), col.reshape(1, NODES * LEAF, NRHS)


def solution(mesh):
    return jax.shard_map(
        body,
        mesh=mesh,
        in_specs=(
            P("blk", "lvl", None),
            P("lvl", None),
            P("blk", "lvl", None, None),
            P("blk", "lvl", None, None),
            P("blk", None, "lvl", None, None, None),
            P("blk", None, "lvl"),
        ),
        out_specs=(P(("lvl", "blk"), None), P("blk", "lvl", None)),
        check_vma=False,
    )
```
